256 devices in a mesh: col: 32 (over z, x_lo, core), lev: 8 (over y, x_hi).
Axes of the slice: x: 4 (x_hi: 2, x_lo: 2; x = x_hi * 2 + x_lo), y: 4, z: 8, core: 2. Of those that a mesh axis runs over, the one named last changes fastest.
Arguments:
- ensemble: float32 [80, 4, 16, 16384], P(None, None, 'lev', 'col'), may hold values from -60 to 60
- obs_weight: float32 [4, 4, 16, 1024], P(None, None, 'lev'), may hold values from -0.75 to 0.75
- obs_value: float32 [4, 1024], replicated, may hold values from -6 to 6
- obs_tile: int32 [4, 1024, 1], replicated, may hold values from 0 to 31; in each aligned block of 1024 rows (0 to 1023, 1024 to 2047, ..., all dimensions but the last counted through in order) at most 128 rows name the same one
- obs_offset: int32 [4, 1024], replicated, may hold values from 0 to 511
- obs_gain: bfloat16 [4, 1024, 1024], P(None, 'lev'), may hold values from -0.1 to 0.3
- localize: bfloat16 [4, 1024, 16384], P(None, None, 'col'), may hold values from 0.049804688 to 1
Outputs:
- analysis: float32 [80, 4, 16, 16384], P(None, None, 'lev', 'col')
The draws below stay inside these ranges and needn't reach their ends.
Inputs may be any that keep to these rules, and one draw needn't show every extreme that they name: `obs_tile`: in each batch at most 128 observations lie in one column tile; in some batch some tile holds exactly 128.
All inputs are finite; a program needn't handle non-finite values.
Results may differ from the reference program's by a relative error of at most 0.012.
The reference program's roundings to bfloat16 on the way (of `innovation`, `increment`, `anom_short`, `state_anom` and `coefficient`) count: a program that leaves them out, or rounds other values in their place, can miss the bound.
Values may be sent and summed in bfloat16 or wider, within the bound.
A program may use at most 64 MiB of HBM per device.

```python
import math
import jax
import jax.numpy as jnp
import numpy as np
from jax import lax

MEMBERS = 80
FIELDS = 4
COL_DEV = 512
NOBS = 1024
BATCHES = 4
LEVELS = 16
NCOL = 16384
CAP = 128
N_COL = 32


def draw_ensemble(key, part):
    key = jax.random.fold_in(key, 11)
    key_noise, key_spread = jax.random.split(key, 2)
    full_shape = (MEMBERS, FIELDS, LEVELS, NCOL)
    spread = jnp.exp(jax.random.uniform(key_spread, (1, FIELDS, LEVELS, NCOL), jnp.float32, -1.15, 1.15))
    noise = jnp.clip(jax.random.normal(key_noise, full_shape, jnp.float32), -5.0, 5.0)
    return (spread * noise).astype(jnp.float32)


def draw_obs_gain(key, part):
    key = jax.random.fold_in(key, 23)
    key_diag, key_off = jax.random.split(key, 2)
    full_shape = (BATCHES, NOBS, NOBS)
    row_index = lax.broadcasted_iota(jnp.int32, full_shape, 1)
    col_index = lax.broadcasted_iota(jnp.int32, full_shape, 2)
    diagonal = jax.random.uniform(key_diag, full_shape, jnp.float32, 0.1, 0.298)
    off_diag = jnp.clip(jax.random.normal(key_off, full_shape, jnp.float32), -6.0, 6.0) * (0.1 / math.sqrt(NOBS))
    return jnp.where(row_index == col_index, diagonal, off_diag).astype(jnp.bfloat16)


def with_ends(drawn, key, low, top_value):
    place = [jax.random.randint(jax.random.fold_in(key, axis), (), 0, length) for axis, length in enumerate(drawn.shape)]
    widest = drawn.shape.index(max(drawn.shape))
    next_to = place[:widest] + [(place[widest] + 1) % drawn.shape[widest]] + place[widest + 1:]
    return drawn.at[tuple(place)].set(low).at[tuple(next_to)].set(top_value)


def shard_levels(rng, dims, pieces, least, largest):
    factor_of, own = 1.0, jax.random.fold_in(rng, 6)
    for axis_at, shards_of in pieces:
        draws = jnp.exp(jax.random.uniform(jax.random.fold_in(own, axis_at), (shards_of,), jnp.float32, least / len(pieces), largest / len(pieces)))
        factor_of = factor_of * jnp.repeat(draws, dims[axis_at] // shards_of).reshape([-1 if axis == axis_at else 1 for axis in range(len(dims))])
    return factor_of


def deal_out(own_key, own, number, rows, number_of, top, most, slope):
    order = jax.random.permutation(own_key, number_of)
    crowded, usual = portions_of(number_of, rows * top, most, slope, True), portions_of(number_of, rows * top, most, slope, False)
    places = jnp.arange(number_of)

    def named(lengths, turn):
        used = int((lengths > 0).sum())
        fixed = max(1, used // 4)
        shifted = fixed + (places - fixed + turn * (used - fixed)) % max(1, number_of - fixed)
        return jnp.zeros((number_of,), jnp.int32).at[order[jnp.where(places < fixed, places, shifted)]].set(jnp.asarray(lengths, jnp.int32))

    lengths = jnp.where(number % 4 == 0, named(crowded, number // 4), named(usual, number - number // 4 - 1))
    mixed = jax.random.permutation(jax.random.fold_in(own, 3), number_of)
    source_of, receiver = mixed[0:number_of // 2 * 2:2], mixed[1:number_of // 2 * 2:2]
    room = jnp.minimum(lengths[source_of] - 1, most - lengths[receiver]) // 2
    room = jnp.where((source_of == order[0]) | (receiver == order[0]) | (lengths[receiver] == 0), 0, jnp.maximum(room, 0))
    shifted = jax.random.randint(jax.random.fold_in(own, 4), (number_of // 2,), 0, 1 << 20) % (room + 1)
    lengths = lengths.at[source_of].add(-shifted).at[receiver].add(shifted)
    items = jnp.searchsorted(jnp.cumsum(lengths), jnp.arange(rows * top), side="right").astype(jnp.int32)
    listing = items.reshape(top, rows).T
    listing = listing[jax.random.permutation(jax.random.fold_in(own, 1), rows)]
    turn = jax.random.randint(jax.random.fold_in(own, 2), (rows, 1), 0, top)
    return jnp.take_along_axis(listing, (jnp.arange(top)[None, :] + turn) % top, axis=1)


def portions_of(count, total, bound, skew, full):
    weights = [(1 << 20) // math.isqrt(grade ** skew) + 1 for grade in range(1, count + 1)]
    largest = bound if full else min(bound, max(-(-total // count), total * weights[0] // sum(weights)))
    least = 1 if total - largest >= count - 1 else 0
    holding, surplus = [largest] + [least] * (count - 1), total - largest - least * (count - 1)
    while surplus > 0:
        free = [i for i in range(1, count) if holding[i] < largest] or [i for i in range(1, count) if holding[i] < bound]
        mass, budget = sum([weights[i] for i in free]), surplus
        for i in free:
            more = min(bound - holding[i], max(1, budget * weights[i] // mass), surplus)
            holding[i] = holding[i] + more
            surplus = surplus - more
    return np.array(holding)


def centred(stream_key, extent, deviation, limit, cuts=(), held_as=jnp.bfloat16):
    values = deviation * jax.random.normal(stream_key, extent, jnp.float32)
    if cuts:
        values = values * shard_levels(stream_key, extent, cuts, -0.22, 0.18)
    return jnp.clip(values, -limit, limit).astype(held_as)


def setup_inputs(seed: int = 0) -> dict:
    arg_keys = jax.random.split(jax.random.key(seed), 8)
    ensemble = draw_ensemble(jax.random.fold_in(arg_keys[7], 71), 0)
    obs_weight = centred(arg_keys[1], (BATCHES, FIELDS, LEVELS, NOBS), (FIELDS * LEVELS) ** -0.5, 0.75, ((2, 8),), jnp.float32)
    obs_value = centred(arg_keys[2], (BATCHES, NOBS), 1.0, 6.0, (), jnp.float32)
    obs_tile_keys = jax.random.split(jax.random.fold_in(arg_keys[3], 1), BATCHES * NOBS // NOBS)
    obs_tile_turns = jax.random.permutation(jax.random.fold_in(arg_keys[3], 3), BATCHES * NOBS // NOBS)
    obs_tile = jax.vmap(lambda own, number: deal_out(jax.random.fold_in(arg_keys[3], 2), own, number, NOBS, N_COL, 1, CAP, 2))(obs_tile_keys, obs_tile_turns).reshape((BATCHES, NOBS, 1))
    obs_offset = with_ends(jax.random.randint(arg_keys[4], (BATCHES, NOBS), 0, COL_DEV), jax.random.fold_in(arg_keys[4], 1), 0, COL_DEV - 1).astype(jnp.int32)
    obs_gain = draw_obs_gain(jax.random.fold_in(arg_keys[7], 71), 0)
    localize = jnp.clip(jnp.exp(math.log(1.0) - 2.9996462 * jax.random.uniform(arg_keys[6], (BATCHES, NOBS, NCOL), jnp.float32) ** shard_levels(arg_keys[6], (BATCHES, NOBS, NCOL), ((2, 32),), -0.2, 0.2)), 0.049804688, 1.0).astype(jnp.bfloat16)
    return {"ensemble": ensemble, "obs_weight": obs_weight, "obs_value": obs_value, "obs_tile": obs_tile, "obs_offset": obs_offset, "obs_gain": obs_gain, "localize": localize}


def batch_update(current, obs_weight, obs_value, tile_ids, offsets, obs_gain, localize):
    members = current.shape[0]
    columns = (tile_ids[:, 0] * COL_DEV + offsets).astype(jnp.int32)
    picked = jnp.take(current, columns, axis=3)
    prior_ens = jnp.sum(picked * obs_weight[None], axis=(1, 2))
    prior_mean = jnp.mean(prior_ens, axis=0)
    prior_anom = prior_ens - prior_mean[None]
    variance = jnp.sum(prior_anom * prior_anom, axis=0) / (members - 1) + 1e-6
    innovation = (obs_value[None] - prior_ens).astype(jnp.bfloat16)
    increment = jnp.dot(innovation, obs_gain.T, preferred_element_type=jnp.float32).astype(jnp.bfloat16)
    anom_short = prior_anom.astype(jnp.bfloat16)
    inv_scale = 1.0 / ((members - 1) * variance)
    state_anom = (current - jnp.mean(current, axis=0)[None]).astype(jnp.bfloat16)
    block_count = NCOL // COL_DEV
    shaped = jnp.moveaxis(state_anom.reshape(members, FIELDS, LEVELS, block_count, COL_DEV), 3, 0)
    loc_blocks = jnp.moveaxis(localize.reshape(NOBS, block_count, COL_DEV), 1, 0)

    def one_block(operands):
        anom_block, loc_block = operands
        flattened = anom_block.reshape(members, -1)
        covariance = jnp.dot(anom_short.T, flattened, preferred_element_type=jnp.float32)
        covariance = covariance.reshape(NOBS, FIELDS * LEVELS, COL_DEV)
        coefficient = (covariance * inv_scale[:, None, None] * loc_block[:, None, :]).astype(jnp.bfloat16)
        change = jnp.dot(increment, coefficient.reshape(NOBS, -1), preferred_element_type=jnp.float32)
        return change.reshape(members, FIELDS, LEVELS, COL_DEV)

    changes = lax.map(one_block, (shaped, loc_blocks))
    changes = jnp.moveaxis(changes, 0, 3).reshape(current.shape)
    return current + changes


def reference(ensemble, obs_weight, obs_value, obs_tile, obs_offset, obs_gain, localize):
    current = ensemble
    for batch_index in range(BATCHES):
        current = batch_update(current, obs_weight[batch_index], obs_value[batch_index], obs_tile[batch_index], obs_offset[batch_index], obs_gain[batch_index], localize[batch_index])
    return current
```

```python
import jax
import jax.numpy as jnp
from jax import lax
from jax.experimental import pallas as pl
from jax.experimental.pallas import tpu as pltpu
from jax.sharding import PartitionSpec as P

F32, BF16, I32 = jnp.float32, jnp.bfloat16, jnp.int32
MESH = pl.DeviceIdType.MESH
MEMBERS = 80
PAD = 128
NB = 4
NOBS = 1024
NCOL, NLEV = 32, 8
FL = 8
WIDTH = 512


def iota(shape, axis):
    return lax.broadcasted_iota(I32, shape, axis)


def dot(a, b):
    return lax.dot_general(a, b, (((1,), (0,)), ((), ())), preferred_element_type=F32)


def dot_nt(a, b):
    return lax.dot_general(a, b, (((1,), (1,)), ((), ())), preferred_element_type=F32)


def parts(x, count):
    out = []
    for _ in range(count):
        piece = x.astype(BF16)
        out.append(piece)
        x = x - piece.astype(F32)
    return out


def wait_bytes(ref, sem):
    pltpu.make_async_copy(ref, ref, sem).wait()


def loop(count, body):
    lax.fori_loop(0, count, lambda k, c: (body(k), c)[1], 0)


def kernel(
    tile_ref, off_ref, val_ref, w_ref, ens_hbm, gain_hbm, loc_hbm, out_hbm,
    cur, gain, loc, oh, x, xt, xn, xa, rs, zs, zr, inn, an, inc, perm, gainp, lsel,
    aj, locs, dhi, dlo, sa, coef, gcol, wsl, cmat, ovs,
    in_sem, out_sem, rs_s, rs_r, ag_s, ag_r, z_s, z_r, wi_s, wi_r, wa_s, wa_r,
    fi_s, fi_r, fa_s, fa_r, ic_s, ic_r,
):
    col, lev = lax.axis_index("col"), lax.axis_index("lev")
    z, quad = col // 4, col % 4
    x_lo, core = quad // 2, quad % 2
    sibling = col + 1 - 2 * core
    spot = lev * 2 + x_lo
    rho = core * 16 + spot

    loads = [pltpu.make_async_copy(ens_hbm, cur, in_sem.at[0]),
             pltpu.make_async_copy(gain_hbm, gain, in_sem.at[1])]
    loads += [pltpu.make_async_copy(loc_hbm.at[b], loc.at[b], in_sem.at[2 + b]) for b in range(NB)]
    for load in loads:
        load.start()

    def chip(k):
        other = lax.rem(spot + k, 16)
        return z * 4 + (other % 2) * 2 + core, other // 2

    barrier = pltpu.get_barrier_semaphore()

    def greet_col(k):
        pl.semaphore_signal(barrier, inc=1, device_id={"col": lax.rem(col + k + 1, NCOL), "lev": lev}, device_id_type=MESH)

    def greet_chip(k):
        c, l = chip(k + 1)
        pl.semaphore_signal(barrier, inc=1, device_id={"col": c, "lev": l}, device_id_type=MESH)

    loop(NCOL - 1, greet_col)
    loop(15, greet_chip)

    tiles = tile_ref[...]
    member_of = jnp.concatenate(
        [jnp.where(tiles[b:b + 1, :] == iota((NCOL, NOBS), 0), 1.0, 0.0) for b in range(NB)], axis=0)
    member_b = member_of.astype(BF16)
    upper = jnp.where(iota((256, 256), 0) < iota((256, 256), 1), 1.0, 0.0).astype(BF16)
    ones = jnp.ones((256, 256), BF16)
    before, total = [], jnp.zeros((128, 256), F32)
    for k in range(4):
        block = member_b[:, 256 * k:256 * (k + 1)]
        before.append(dot(block, upper) + total)
        total = total + dot(block, ones)
    before = jnp.concatenate(before, axis=1)
    row, lane = iota((128, 128), 0), iota((128, 128), 1)
    lower = jnp.where((row // 32 == lane // 32) & (lane < row), 1.0, 0.0).astype(BF16)
    start = dot(lower, total[:, :128].astype(BF16))[:, :1]
    g_rows, code_rows = [], []
    for b in range(NB):
        mine = member_of[32 * b:32 * b + 32]
        begin = start[32 * b:32 * b + 32]
        g = jnp.sum(mine * (before[32 * b:32 * b + 32] + begin), axis=0, keepdims=True)
        g_rows.append(g)
        gi = g.astype(I32)
        first = jnp.sum(mine * begin, axis=0, keepdims=True).astype(I32)
        res = gi & 31
        rank = (gi >> 5) - ((first - res + 31) >> 5)
        slot = 16 * ((res >> 1) & 7) + 8 * (res & 1) + 4 * (res >> 4) + rank
        code_rows.append(jnp.where(tiles[b:b + 1, :] == col, slot, -1))
    gcol[...] = jnp.concatenate(g_rows + [jnp.zeros((4, NOBS), F32)], axis=0).T

    for b in range(NB):
        pick = jnp.where(code_rows[b] == iota((PAD, NOBS), 0), 1.0, 0.0).astype(BF16)
        off = off_ref[b:b + 1, :]
        head = jnp.concatenate(
            [(off >> 8).astype(F32), (off & 255).astype(F32), jnp.ones((1, NOBS), F32), jnp.zeros((5, NOBS), F32)], axis=0)
        wp = [p.astype(F32) for p in parts(w_ref[b], 3)]
        got = dot_nt(jnp.concatenate([head] + wp, axis=0).astype(BF16), pick)
        column = got[0:1] * 256.0 + got[1:2] + (got[2:3] - 1.0) * 10000.0
        wsl[:, 128 * b:128 * b + 128] = got[8:16] + got[16:24] + got[24:32]
        oh[:, 128 * b:128 * b + 128] = jnp.where(
            iota((WIDTH, PAD), 0) == column.astype(I32), 1.0, 0.0).astype(BF16)

    x[...] = jnp.zeros_like(x)
    loads[0].wait()

    def project(fl):
        got = dot(jnp.concatenate(parts(cur[fl], 3), axis=0), oh[...])
        x[0:MEMBERS, :] += (got[0:80] + got[80:160] + got[160:240]) * wsl[pl.ds(fl, 1), :]

    loop(FL, project)
    for b in range(NB):
        xt[b] = x[:, 128 * b:128 * b + 128].T.reshape(NLEV, 16, PAD)

    pl.semaphore_wait(barrier, NCOL - 1 + 15)

    def lev_peer(k):
        return lax.rem(lev + k + 1, NLEV)

    def send_first(k):
        to = lev_peer(k)
        pltpu.make_async_remote_copy(
            src_ref=xt.at[0, to], dst_ref=rs.at[lev, 0], send_sem=rs_s.at[0], recv_sem=rs_r.at[0],
            device_id={"col": col, "lev": to}, device_id_type=MESH).start()

    def send_rest(k):
        to = lev_peer(k)
        pltpu.make_async_remote_copy(
            src_ref=xt.at[pl.ds(1, 3), to], dst_ref=rs.at[lev, pl.ds(1, 3)], send_sem=rs_s.at[1], recv_sem=rs_r.at[1],
            device_id={"col": col, "lev": to}, device_id_type=MESH).start()

    loop(NLEV - 1, send_first)
    loop(NLEV - 1, send_rest)

    def place(b):
        want = ((iota((256, NOBS), 1) & 31) * 32 + (iota((256, NOBS), 1) >> 5)).astype(F32)

        def rows(k):
            at = pl.ds(pl.multiple_of(k * 256, 256), 256)
            perm[b % 2, at, :] = jnp.where(gcol[at, b:b + 1] == want, 1.0, 0.0).astype(BF16)

        loop(4, rows)
        gainp[b % 2] = dot(gain[b], perm[b % 2]).astype(BF16)

    def select(b):
        if b == NB - 1:
            return
        if b == 0:
            for load in loads[2:]:
                load.wait()
        wide = 128 * (NB - 1 - b)

        def rows(k):
            at = pl.ds(pl.multiple_of(k * 256, 256), 256)
            lsel[at, 0:wide] = dot(loc[b, at, :], oh[:, 128 * (b + 1):])

        loop(4, rows)

    def anomaly(fl):
        block = cur[fl]
        sa[fl, 0:MEMBERS, :] = (block - jnp.mean(block, axis=0, keepdims=True)).astype(BF16)

    def send_z(b):
        for k in range(4):
            zs[b, k] = xn[b, lev, 4 * k:4 * k + 4, :]
        zr[b, col] = zs[b, quad]

        def one(k):
            to = lax.rem(col + k + 1, NCOL)
            pltpu.make_async_remote_copy(
                src_ref=zs.at[b, to % 4], dst_ref=zr.at[b, col], send_sem=z_s.at[b], recv_sem=z_r.at[b],
                device_id={"col": to, "lev": lev}, device_id_type=MESH).start()

        loop(NCOL - 1, one)

    counts = dot_nt(jnp.ones((8, NOBS), BF16), member_b)
    own_batch = iota((8, 128), 1) // 32 == iota((8, 128), 0)
    counts = jnp.where(own_batch, counts, 0.0).astype(BF16)
    tile_row, tile_lane = iota((128, 128), 0) % 32, iota((128, 128), 1) // 4
    begins = dot(counts, jnp.where(tile_row < tile_lane, 1.0, 0.0).astype(BF16)).astype(I32)
    ends = dot(counts, jnp.where(tile_row <= tile_lane, 1.0, 0.0).astype(BF16)).astype(I32)
    q = iota((32, 128), 0)
    for b in range(NB):
        want = (iota((32, 128), 1) & 3) + ((begins[b:b + 1] - rho + 31) >> 5)
        cmat[b] = jnp.where((q == want) & (32 * q + rho < ends[b:b + 1]), 1.0, 0.0).astype(BF16)
        here = g_rows[b].astype(I32) == 32 * iota((32, NOBS), 0) + rho
        ovs[b] = jnp.broadcast_to(jnp.sum(jnp.where(here, val_ref[b:b + 1, :], 0.0), axis=1, keepdims=True), (32, PAD))

    sa[...] = jnp.zeros_like(sa)
    loads[1].wait()
    place(0)

    wait_bytes(rs.at[pl.ds(0, 7), 0], rs_r.at[0])
    rs[lev, 0] = xt[0, lev]
    xn[0, lev] = jnp.sum(rs[:, 0], axis=0)
    send_z(0)

    wait_bytes(rs.at[pl.ds(0, 7), pl.ds(1, 3)], rs_r.at[1])
    for b in range(1, NB):
        rs[lev, b] = xt[b, lev]
        xa[b - 1, lev] = jnp.sum(rs[:, b], axis=0)

    def send_xa(k):
        to = lev_peer(k)
        pltpu.make_async_remote_copy(
            src_ref=xa.at[:, lev], dst_ref=xa.at[:, lev], send_sem=ag_s, recv_sem=ag_r,
            device_id={"col": col, "lev": to}, device_id_type=MESH).start()

    loop(NLEV - 1, send_xa)
    select(0)
    loop(FL, anomaly)

    lane_of = iota((32, PAD), 1)
    in_members = lane_of < MEMBERS

    def spread(buf, b, s_sem, r_sem):
        own = buf.at[b, pl.ds(pl.multiple_of(rho * 32, 32), 32)]

        def one(k):
            c, l = chip(k + 1)
            pltpu.make_async_remote_copy(
                src_ref=own, dst_ref=own, send_sem=s_sem.at[b], recv_sem=r_sem.at[b],
                device_id={"col": c, "lev": l}, device_id_type=MESH).start()

        loop(15, one)

    def forward(buf, b, r_sem, fs_sem, fr_sem):
        wait_bytes(buf.at[b, pl.ds(0, 480)], r_sem.at[b])
        half = buf.at[b, pl.ds(pl.multiple_of(core * 512, 512), 512)]
        pltpu.make_async_remote_copy(
            src_ref=half, dst_ref=half, send_sem=fs_sem.at[b], recv_sem=fr_sem.at[b],
            device_id={"col": sibling, "lev": lev}, device_id_type=MESH).start()

    def cov(b, fl):
        for h in range(2):
            at = slice(256 * h, 256 * h + 256)
            got = dot(aj[...], sa[fl, :, at]) * locs[:, at]
            coef[fl, :, at] = got.astype(BF16)

    def change(b, fl):
        cur[fl] += dot(inc[b], coef[fl])

    def out_copy(fl):
        return pltpu.make_async_copy(cur.at[fl], out_hbm.at[fl], out_sem)

    for b in range(NB):
        if b > 0:
            loop(FL, lambda fl: change(b - 1, fl))
        wait_bytes(zr.at[b, pl.ds(0, NCOL - 1)], z_r.at[b])
        got = zr[b].reshape(128, PAD)
        hi, lo = parts(got, 2)
        prior = dot(cmat[b], hi) + dot(cmat[b], lo)
        mean = jnp.sum(prior, axis=1, keepdims=True) * (1.0 / MEMBERS)
        anom = jnp.where(in_members, prior - mean, 0.0)
        variance = jnp.sum(anom * anom, axis=1, keepdims=True) / (MEMBERS - 1) + 1e-6
        scale = parts(1.0 / ((MEMBERS - 1) * variance), 3)
        mine = pl.ds(pl.multiple_of(rho * 32, 32), 32)
        inn[b, mine, :] = jnp.where(in_members, ovs[b] - prior, 0.0).astype(BF16)
        spread(inn, b, wi_s, wi_r)
        for k in range(3):
            anom = jnp.where(lane_of == MEMBERS + k, scale[k].astype(F32), anom)
        an[b, mine, :] = anom.astype(BF16)
        spread(an, b, wa_s, wa_r)
        if b == 0:
            wait_bytes(xa.at[:, pl.ds(0, 7)], ag_r)
            for k in range(1, NB):
                x[:, 128 * k:128 * k + 128] = xa[k - 1].reshape(128, PAD).T
        else:
            loop(FL, anomaly)
        forward(inn, b, wi_r, fi_s, fi_r)
        forward(an, b, wa_r, fa_s, fa_r)
        if b + 1 < NB:
            place(b + 1)
        wait_bytes(inn.at[b, pl.ds(0, 512)], fi_r.at[b])
        rows = dot(gainp[b % 2], inn[b])
        own = pl.ds(pl.multiple_of(lev * 128, 128), 128)
        inc[b, :, own] = rows.T[0:MEMBERS].astype(BF16)

        def send_inc(k):
            piece = inc.at[b, :, own]
            pltpu.make_async_remote_copy(
                src_ref=piece, dst_ref=piece, send_sem=ic_s.at[b], recv_sem=ic_r.at[b],
                device_id={"col": col, "lev": lev_peer(k)}, device_id_type=MESH).start()

        loop(NLEV - 1, send_inc)
        wait_bytes(an.at[b, pl.ds(0, 512)], fa_r.at[b])
        wide = 128 * (NB - 1 - b)
        if b + 1 < NB:
            future = x[:, 128 * (b + 1):]
            keep = iota((PAD, wide), 0) < MEMBERS
            future = jnp.where(keep, future - jnp.sum(future, axis=0, keepdims=True) * (1.0 / MEMBERS), 0.0)
            xh, xl = parts(future, 2)

        def unpack(k):
            at = pl.ds(pl.multiple_of(k * 256, 256), 256)
            got = dot(perm[b % 2, at, :], an[b])
            scale_col = got[:, 80:81] + got[:, 81:82] + got[:, 82:83]
            short = got.astype(BF16)
            aj[at, :] = short
            locs[at, :] = loc[b, at, :].astype(F32) * scale_col
            if b + 1 < NB:
                d = (dot(short, xh) + dot(short, xl)) * (lsel[at, 0:wide] * scale_col)
                high, low = parts(d, 2)
                dhi[at, 0:wide] = high
                dlo[at, 0:wide] = low

        loop(4, unpack)
        if b + 1 < NB:
            select(b + 1)
        loop(FL, lambda fl: cov(b, fl))
        wait_bytes(inc.at[b, :, pl.ds(0, 896)], ic_r.at[b])
        if b + 1 < NB:
            nxt = slice(128 * (b + 1), 128 * (b + 2))
            fresh = x[0:MEMBERS, nxt] + dot(inc[b], dhi[:, 0:128]) + dot(inc[b], dlo[:, 0:128])
            x[0:MEMBERS, nxt] = fresh
            xn[b + 1] = x[:, nxt].T.reshape(NLEV, 16, PAD)
            send_z(b + 1)
        if b + 2 < NB:
            later = slice(128 * (b + 2), 128 * NB)
            x[0:MEMBERS, later] += dot(inc[b], dhi[:, 128:wide]) + dot(inc[b], dlo[:, 128:wide])

    def finish(fl):
        change(NB - 1, fl)
        out_copy(fl).start()

    loop(FL, finish)
    wait_bytes(cur, out_sem)
    wait_bytes(rs.at[pl.ds(0, 7), 0], rs_s.at[0])
    wait_bytes(rs.at[pl.ds(0, 7), pl.ds(1, 3)], rs_s.at[1])
    wait_bytes(xa.at[:, pl.ds(0, 7)], ag_s)
    for b in range(NB):
        wait_bytes(zr.at[b, pl.ds(0, NCOL - 1)], z_s.at[b])
        wait_bytes(inn.at[b, pl.ds(0, 480)], wi_s.at[b])
        wait_bytes(an.at[b, pl.ds(0, 480)], wa_s.at[b])
        wait_bytes(inn.at[b, pl.ds(0, 512)], fi_s.at[b])
        wait_bytes(an.at[b, pl.ds(0, 512)], fa_s.at[b])
        wait_bytes(inc.at[b, :, pl.ds(0, 896)], ic_s.at[b])


def shards(ensemble, obs_weight, obs_value, obs_tile, obs_offset, obs_gain, localize):
    state = jnp.transpose(ensemble, (1, 2, 0, 3)).reshape(FL, MEMBERS, WIDTH)
    vmem, hbm = pl.BlockSpec(memory_space=pltpu.VMEM), pl.BlockSpec(memory_space=pl.ANY)
    dma = pltpu.SemaphoreType.DMA
    out = pl.pallas_call(
        kernel,
        out_shape=jax.ShapeDtypeStruct((FL, MEMBERS, WIDTH), F32),
        in_specs=[vmem] * 4 + [hbm] * 3,
        out_specs=hbm,
        scratch_shapes=[
            pltpu.VMEM((FL, MEMBERS, WIDTH), F32),
            pltpu.VMEM((NB, 128, NOBS), BF16),
            pltpu.VMEM((NB, NOBS, WIDTH), BF16),
            pltpu.VMEM((WIDTH, NB * 128), BF16),
            pltpu.VMEM((PAD, NB * 128), F32),
            pltpu.VMEM((NB, NLEV, 16, PAD), F32),
            pltpu.VMEM((NB, NLEV, 16, PAD), F32),
            pltpu.VMEM((NB - 1, NLEV, 16, PAD), F32),
            pltpu.VMEM((NLEV, NB, 16, PAD), F32),
            pltpu.VMEM((NB, 4, 4, PAD), F32),
            pltpu.VMEM((NB, NCOL, 4, PAD), F32),
            pltpu.VMEM((NB, NOBS, PAD), BF16),
            pltpu.VMEM((NB, NOBS, PAD), BF16),
            pltpu.VMEM((NB, MEMBERS, NOBS), BF16),
            pltpu.VMEM((2, NOBS, NOBS), BF16),
            pltpu.VMEM((2, 128, NOBS), BF16),
            pltpu.VMEM((NOBS, 384), F32),
            pltpu.VMEM((NOBS, PAD), BF16),
            pltpu.VMEM((NOBS, WIDTH), F32),
            pltpu.VMEM((NOBS, 384), BF16),
            pltpu.VMEM((NOBS, 384), BF16),
            pltpu.VMEM((FL, PAD, WIDTH), BF16),
            pltpu.VMEM((FL, NOBS, WIDTH), BF16),
            pltpu.VMEM((NOBS, 8), F32),
            pltpu.VMEM((8, NB * 128), F32),
            pltpu.VMEM((NB, 32, 128), BF16),
            pltpu.VMEM((NB, 32, PAD), F32),
            dma((6,)), dma, dma((2,)), dma((2,)), dma, dma,
            dma((NB,)), dma((NB,)), dma((NB,)), dma((NB,)), dma((NB,)), dma((NB,)),
            dma((NB,)), dma((NB,)), dma((NB,)), dma((NB,)), dma((NB,)), dma((NB,)),
        ],
        compiler_params=pltpu.CompilerParams(
            collective_id=0, has_side_effects=True, vmem_limit_bytes=56 * 1024 * 1024),
        cost_estimate=pl.CostEstimate(flops=8 * 335544320, bytes_accessed=8 * 1024 * 1024, transcendentals=0),
    )(
        obs_tile[:, :, 0], obs_offset, obs_value, obs_weight.reshape(NB, FL, NOBS), state, obs_gain, localize,
    )
    return jnp.transpose(out.reshape(4, 2, MEMBERS, WIDTH), (2, 0, 1, 3))


def solution(mesh):
    in_specs = (
        P(None, None, "lev", "col"),
        P(None, None, "lev", None),
        P(),
        P(),
        P(),
        P(None, "lev", None),
        P(None, None, "col"),
    )
    out_specs = P(None, None, "lev", "col")
    return jax.shard_map(shards, mesh=mesh, in_specs=in_specs, out_specs=out_specs, check_vma=False)
```

```python
import jax
import jax.numpy as jnp
from jax import lax
from jax.experimental import pallas as pl
from jax.experimental.pallas import tpu as pltpu
from jax.sharding import PartitionSpec as P

F32, BF16, I32 = jnp.float32, jnp.bfloat16, jnp.int32
MESH = pl.DeviceIdType.MESH
MEMBERS = 80
PAD = 128
NB = 4
NOBS = 1024
NCOL, NLEV = 32, 8
FL = 8
WIDTH = 512


def iota(shape, axis):
    return lax.broadcasted_iota(I32, shape, axis)


def dot(a, b):
    return lax.dot_general(a, b, (((1,), (0,)), ((), ())), preferred_element_type=F32)


def dot_nt(a, b):
    return lax.dot_general(a, b, (((1,), (1,)), ((), ())), preferred_element_type=F32)


def parts(x, count):
    out = []
    for _ in range(count):
        piece = x.astype(BF16)
        out.append(piece)
        x = x - piece.astype(F32)
    return out


def wait_bytes(ref, sem):
    pltpu.make_async_copy(ref, ref, sem).wait()


def push(src, dst, s_sem, r_sem, col, lev):
    pltpu.make_async_remote_copy(
        src_ref=src, dst_ref=dst, send_sem=s_sem, recv_sem=r_sem,
        device_id={"col": col, "lev": lev}, device_id_type=MESH).start()


def loop(count, body):
    lax.fori_loop(0, count, lambda k, c: (body(k), c)[1], 0)


def kernel(
    tile_ref, off_ref, val_ref, w_ref, ens_hbm, gain_hbm, loc_hbm, out_hbm,
    raw, cur, gain, loc, oh, x, xt, got_t, own, rs, zs, zr, ls, lsend, lrecv, later, inn, an, inc, perm, gainp,
    aj, locs, dt, sa, coef, gcol, wsl, cmat, cbig, ovs,
    in_sem, out_sem, rs_s, rs_r, z_s, z_r, l_s, l_r, wi_s, wi_r, wa_s, wa_r,
    fi_s, fi_r, fa_s, fa_r, ic_s, ic_r,
):
    col, lev = lax.axis_index("col"), lax.axis_index("lev")
    z, quad = col // 4, col % 4
    x_lo, core = quad // 2, quad % 2
    sibling = col + 1 - 2 * core
    spot = lev * 2 + x_lo
    rho = core * 16 + spot

    loads = [pltpu.make_async_copy(ens_hbm, raw, in_sem.at[0]),
             pltpu.make_async_copy(gain_hbm, gain, in_sem.at[1])]
    loads += [pltpu.make_async_copy(loc_hbm.at[b], loc.at[b], in_sem.at[2 + b]) for b in range(NB)]
    for load in loads:
        load.start()

    def chip(k):
        other = lax.rem(spot + k, 16)
        return z * 4 + (other % 2) * 2 + core, other // 2

    barrier = pltpu.get_barrier_semaphore()

    def greet_col(k):
        pl.semaphore_signal(barrier, inc=1, device_id={"col": lax.rem(col + k + 1, NCOL), "lev": lev}, device_id_type=MESH)

    def greet_chip(k):
        c, l = chip(k + 1)
        pl.semaphore_signal(barrier, inc=1, device_id={"col": c, "lev": l}, device_id_type=MESH)

    loop(NCOL - 1, greet_col)
    loop(15, greet_chip)

    tiles = [tile_ref[b] for b in range(NB)]
    member_of = jnp.concatenate(
        [jnp.where(tiles[b] == iota((NCOL, NOBS), 0), 1.0, 0.0) for b in range(NB)], axis=0)
    member_b = member_of.astype(BF16)
    upper = jnp.where(iota((256, 256), 0) < iota((256, 256), 1), 1.0, 0.0).astype(BF16)
    ones = jnp.ones((256, 256), BF16)
    before, total = [], jnp.zeros((128, 256), F32)
    for k in range(4):
        block = member_b[:, 256 * k:256 * (k + 1)]
        before.append(dot(block, upper) + total)
        total = total + dot(block, ones)
    before = jnp.concatenate(before, axis=1)
    row, lane = iota((128, 128), 0), iota((128, 128), 1)
    lower = jnp.where((row // 32 == lane // 32) & (lane < row), 1.0, 0.0).astype(BF16)
    start = dot(lower, total[:, :128].astype(BF16))[:, :1]
    g_rows, code_rows = [], []
    for b in range(NB):
        mine = member_of[32 * b:32 * b + 32]
        begin = start[32 * b:32 * b + 32]
        g = jnp.sum(mine * (before[32 * b:32 * b + 32] + begin), axis=0, keepdims=True)
        g_rows.append(g)
        gi = g.astype(I32)
        first = jnp.sum(mine * begin, axis=0, keepdims=True).astype(I32)
        res = gi & 31
        rank = (gi >> 5) - ((first - res + 31) >> 5)
        slot = 16 * ((res >> 1) & 7) + 8 * (res & 1) + 4 * (res >> 4) + rank
        code_rows.append(jnp.where(tiles[b] == col, slot, -1))

    for b in range(NB):
        pick = jnp.where(code_rows[b] == iota((PAD, NOBS), 0), 1.0, 0.0).astype(BF16)
        off = off_ref[b:b + 1, :]
        head = jnp.concatenate(
            [(off >> 8).astype(F32), (off & 255).astype(F32), jnp.ones((1, NOBS), F32), jnp.zeros((5, NOBS), F32)], axis=0)
        weights = jnp.concatenate(
            [jnp.concatenate([w_ref[pl.ds(64 * b + 2 * c + l, 4, stride=16), :] for l in range(2)], axis=0)
             for c in range(8)], axis=1)
        wp = [p.astype(F32) for p in parts(weights, 3)]
        got = dot_nt(jnp.concatenate([head] + wp, axis=0).astype(BF16), pick)
        column = got[0:1] * 256.0 + got[1:2] + (got[2:3] - 1.0) * 10000.0
        wsl[:, 128 * b:128 * b + 128] = got[8:16] + got[16:24] + got[24:32]
        oh[:, 128 * b:128 * b + 128] = jnp.where(
            iota((WIDTH, PAD), 0) == column.astype(I32), 1.0, 0.0).astype(BF16)
        got_t[b] = jnp.broadcast_to(column, (8, PAD)).T

    x[...] = jnp.zeros_like(x)
    loads[0].wait()

    def rows_of(fl, c):
        return pl.ds((fl % 4) * 8 + fl // 4 + 2 * c, MEMBERS, stride=32)

    def project(fl):
        block = jnp.concatenate([raw[rows_of(fl, c), :] for c in range(4)], axis=1)
        cur[fl] = block
        sa[fl, 0:MEMBERS, :] = (block - jnp.mean(block, axis=0, keepdims=True)).astype(BF16)
        got = dot(jnp.concatenate(parts(block, 3), axis=0), oh[...])
        x[0:MEMBERS, :] += (got[0:80] + got[80:160] + got[160:240]) * wsl[pl.ds(fl, 1), :]

    sa[...] = jnp.zeros_like(sa)
    loop(FL, project)
    for b in range(NB):
        xt[b] = x[:, 128 * b:128 * b + 128].T.reshape(NLEV, 16, PAD)

    pl.semaphore_wait(barrier, NCOL - 1 + 15)

    def lev_peer(k):
        return lax.rem(lev + k + 1, NLEV)

    def send_first(k):
        to = lev_peer(k)
        push(xt.at[0, to], rs.at[lev, 0], rs_s.at[0], rs_r.at[0], col, to)

    def send_rest(k):
        to = lev_peer(k)
        push(xt.at[pl.ds(1, 3), to], rs.at[lev, pl.ds(1, 3)], rs_s.at[1], rs_r.at[1], col, to)

    loop(NLEV - 1, send_first)
    loop(NLEV - 1, send_rest)

    gcol[...] = jnp.concatenate(g_rows + [jnp.zeros((4, NOBS), F32)], axis=0).T
    inc[...] = jnp.zeros_like(inc)

    def place(b):
        want = ((iota((256, NOBS), 1) & 31) * 32 + (iota((256, NOBS), 1) >> 5)).astype(F32)

        def rows(k):
            at = pl.ds(pl.multiple_of(k * 256, 256), 256)
            perm[b % 2, at, :] = jnp.where(gcol[at, b:b + 1] == want, 1.0, 0.0).astype(BF16)

        loop(4, rows)
        gainp[b % 2] = dot(gain[b], perm[b % 2]).astype(BF16)

    loads[1].wait()
    place(0)

    mine16 = pl.ds(pl.multiple_of(lev * 16, 16), 16)
    here = [jnp.where(got_t[b, mine16, 0:1].astype(I32) == iota((16, WIDTH), 1), 1.0, 0.0) for b in range(1, NB)]
    for b in range(NB - 1):
        loads[2 + b].wait()
        got = dot_nt(jnp.concatenate(here[b:], axis=0).astype(BF16), loc[b])
        if b + 2 < NB:
            later[b, 0:16 * (NB - 2 - b), :] = got[16:]
        for k in range(4):
            for c in range(8):
                ls[k, c] = got[4 * k:4 * k + 4, 128 * c:128 * c + 128]
        lsend[b] = ls[...].reshape(4, 32, PAD).astype(BF16)

    counts = dot_nt(jnp.ones((8, NOBS), BF16), member_b)
    counts = jnp.where(iota((8, 128), 1) // 32 == iota((8, 128), 0), counts, 0.0).astype(BF16)

    def edges(lanes, per_tile):
        at, of = iota((128, lanes), 0) % 32, iota((128, lanes), 1) // per_tile
        low = dot(counts, jnp.where(at < of, 1.0, 0.0).astype(BF16)).astype(I32)
        high = dot(counts, jnp.where(at <= of, 1.0, 0.0).astype(BF16)).astype(I32)
        return low, high

    low, high = edges(128, 4)
    q = iota((32, 128), 0)
    for b in range(NB):
        want = (iota((32, 128), 1) & 3) + ((low[b:b + 1] - rho + 31) >> 5)
        cmat[b] = jnp.where((q == want) & (32 * q + rho < high[b:b + 1]), 1.0, 0.0).astype(BF16)
        is_here = g_rows[b].astype(I32) == 32 * iota((32, NOBS), 0) + rho
        ovs[b] = jnp.broadcast_to(jnp.sum(jnp.where(is_here, val_ref[b:b + 1, :], 0.0), axis=1, keepdims=True), (32, PAD))

    def send_z(b):
        zr[b, col] = zs[b, quad]

        def one(k):
            to = lax.rem(col + k + 1, NCOL)
            push(zs.at[b, to % 4], zr.at[b, col], z_s.at[b], z_r.at[b], to, lev)

        loop(NCOL - 1, one)

    def send_l(b):
        lrecv[b, col] = lsend[b, quad]

        def one(k):
            to = lax.rem(col + k + 1, NCOL)
            push(lsend.at[b, to % 4], lrecv.at[b, col], l_s.at[b], l_r.at[b], to, lev)

        loop(NCOL - 1, one)

    wait_bytes(rs.at[pl.ds(0, 7), 0], rs_r.at[0])
    rs[lev, 0] = xt[0, lev]
    first = jnp.sum(rs[:, 0], axis=0)
    for k in range(4):
        zs[0, k] = first[4 * k:4 * k + 4]
    send_z(0)
    wait_bytes(rs.at[pl.ds(0, 7), pl.ds(1, 3)], rs_r.at[1])
    for b in range(1, NB):
        rs[lev, b] = xt[b, lev]
        own[b] = jnp.sum(rs[:, b], axis=0)
    for k in range(4):
        zs[1, k] = own[1, 4 * k:4 * k + 4]
    send_z(1)
    send_l(0)

    low, high = edges(NOBS, 32)
    row_q, row_c = iota((256, NOBS), 0) % 32, iota((256, NOBS), 0) // 32
    lane_c, lane_r = (iota((256, NOBS), 1) >> 2) & 7, iota((256, NOBS), 1) & 3
    for b in range(1, NB):
        want = lane_r + ((low[b:b + 1] - rho + 31) >> 5)
        hit = (row_q == want) & (row_c == lane_c) & (32 * row_q + rho < high[b:b + 1])
        cbig[b - 1] = jnp.where(hit, 1.0, 0.0).astype(BF16)

    lane_of = iota((32, PAD), 1)
    in_members = lane_of < MEMBERS

    def spread(buf, b, s_sem, r_sem):
        piece = buf.at[b, pl.ds(pl.multiple_of(rho * 32, 32), 32)]

        def one(k):
            c, l = chip(k + 1)
            push(piece, piece, s_sem.at[b], r_sem.at[b], c, l)

        loop(15, one)

    def forward(buf, b, r_sem, fs_sem, fr_sem):
        wait_bytes(buf.at[b, pl.ds(0, 480)], r_sem.at[b])
        half = buf.at[b, pl.ds(pl.multiple_of(core * 512, 512), 512)]
        push(half, half, fs_sem.at[b], fr_sem.at[b], sibling, lev)

    def anomaly(fl):
        block = cur[fl]
        sa[fl, 0:MEMBERS, :] = (block - jnp.mean(block, axis=0, keepdims=True)).astype(BF16)

    def cov(b, fl):
        for h in range(2):
            at = slice(256 * h, 256 * h + 256)
            got = dot(aj[...], sa[fl, :, at]) * locs[:, at]
            coef[fl, :, at] = got.astype(BF16)

    def change(b, fl):
        cur[fl] += dot(inc[b, 0:MEMBERS, :], coef[fl])

    def gather_z(b):
        wait_bytes(zr.at[b, pl.ds(0, NCOL - 1)], z_r.at[b])
        hi, lo = parts(zr[b].reshape(128, PAD), 2)
        return dot(cmat[b], hi) + dot(cmat[b], lo)

    def centred(v):
        mean = jnp.sum(v, axis=1, keepdims=True) * (1.0 / MEMBERS)
        return jnp.where(iota(v.shape, 1) < MEMBERS, v - mean, 0.0)

    prior = gather_z(0)
    for b in range(NB):
        anom = centred(prior)
        mine = pl.ds(pl.multiple_of(rho * 32, 32), 32)
        inn[b, mine, :] = jnp.where(in_members, ovs[b] - prior, 0.0).astype(BF16)
        spread(inn, b, wi_s, wi_r)
        variance = jnp.sum(anom * anom, axis=1, keepdims=True) / (MEMBERS - 1) + 1e-6
        scale = parts(1.0 / ((MEMBERS - 1) * variance), 3)
        for k in range(3):
            anom = jnp.where(lane_of == MEMBERS + k, scale[k].astype(F32), anom)
        an[b, mine, :] = anom.astype(BF16)
        spread(an, b, wa_s, wa_r)
        if b > 0:
            if b + 1 < NB:
                send_z(b + 1)
            loop(FL, lambda fl: change(b - 1, fl))
            loop(FL, anomaly)
        if b + 1 < NB:
            place(b + 1)
        forward(inn, b, wi_r, fi_s, fi_r)
        forward(an, b, wa_r, fa_s, fa_r)
        wait_bytes(inn.at[b, pl.ds(0, 512)], fi_r.at[b])
        rows = dot(gainp[b % 2], inn[b])
        lanes = pl.ds(pl.multiple_of(lev * 128, 128), 128)
        inc[b, 0:MEMBERS, lanes] = rows.T[0:MEMBERS].astype(BF16)

        def send_inc(k):
            piece = inc.at[b, pl.ds(0, MEMBERS), lanes]
            push(piece, piece, ic_s.at[b], ic_r.at[b], col, lev_peer(k))

        loop(NLEV - 1, send_inc)
        if b + 2 < NB:
            send_l(b + 1)
        wait_bytes(an.at[b, pl.ds(0, 512)], fa_r.at[b])

        def unpack(k):
            at = pl.ds(pl.multiple_of(k * 256, 256), 256)
            got = dot(perm[b % 2, at, :], an[b])
            scale_col = got[:, 80:81] + got[:, 81:82] + got[:, 82:83]
            aj[at, :] = got.astype(BF16)
            locs[at, :] = loc[b, at, :].astype(F32) * scale_col

        if b == NB - 1:
            loads[2 + b].wait()
        loop(4, unpack)
        if b + 1 < NB:
            after = 16 * (NB - 2 - b)
            held = gather_z(b + 1)
            wait_bytes(lrecv.at[b, pl.ds(0, NCOL - 1)], l_r.at[b])
            sel = dot(cbig[b], lrecv[b].reshape(NOBS, PAD))
            sel = jnp.concatenate([sel[32 * c:32 * c + 32] for c in range(8)], axis=1)
            if after:
                slots = own[b + 2:NB].reshape(after, PAD)
                held = jnp.concatenate([held, slots], axis=0)
                sel = jnp.concatenate([sel, later[b, 0:after, :]], axis=0)
            xh, xl = parts(centred(held), 2)
            pull = jnp.where((iota((16, PAD), 1) >= MEMBERS) & (iota((16, PAD), 1) < MEMBERS + 3), 1.0, 0.0).astype(BF16)
            count = 32 + after
            got = dot_nt(jnp.concatenate([xh, xl, pull], axis=0), aj[...])
            d = (got[0:count] + got[count:2 * count]) * got[2 * count:2 * count + 1] * sel
            dh, dl = parts(d, 2)
            dt[0:count, :] = dh
            dt[count:2 * count, :] = dl
        loop(FL, lambda fl: cov(b, fl))
        wait_bytes(inc.at[b, pl.ds(0, MEMBERS), pl.ds(0, 896)], ic_r.at[b])
        if b + 1 < NB:
            got = dot_nt(dt[0:2 * count, :], inc[b])
            held = held + got[0:count] + got[count:2 * count]
            prior = held[0:32]
            if after:
                own[b + 2:NB] = held[32:].reshape(NB - 2 - b, 16, PAD)
                for k in range(4):
                    zs[b + 2, k] = held[32 + 4 * k:36 + 4 * k]

    def finish(fl):
        block = cur[fl] + dot(inc[NB - 1, 0:MEMBERS, :], coef[fl])
        for c in range(4):
            raw[rows_of(fl, c), :] = block[:, 128 * c:128 * c + 128]

    loop(FL, finish)
    done = pltpu.make_async_copy(raw, out_hbm, out_sem)
    done.start()
    wait_bytes(rs.at[pl.ds(0, 7), 0], rs_s.at[0])
    wait_bytes(rs.at[pl.ds(0, 7), pl.ds(1, 3)], rs_s.at[1])
    for b in range(NB):
        wait_bytes(zr.at[b, pl.ds(0, NCOL - 1)], z_s.at[b])
        if b + 1 < NB:
            wait_bytes(lrecv.at[b, pl.ds(0, NCOL - 1)], l_s.at[b])
        wait_bytes(inn.at[b, pl.ds(0, 480)], wi_s.at[b])
        wait_bytes(an.at[b, pl.ds(0, 480)], wa_s.at[b])
        wait_bytes(inn.at[b, pl.ds(0, 512)], fi_s.at[b])
        wait_bytes(an.at[b, pl.ds(0, 512)], fa_s.at[b])
        wait_bytes(inc.at[b, pl.ds(0, MEMBERS), pl.ds(0, 896)], ic_s.at[b])
    done.wait()


def shards(ensemble, obs_weight, obs_value, obs_tile, obs_offset, obs_gain, localize):
    state = ensemble.reshape(MEMBERS, 4, 2, 4, 128).transpose(0, 1, 3, 2, 4).reshape(MEMBERS * 32, 128)
    weights = obs_weight.reshape(NB, 4, 2, 8, 128).transpose(0, 1, 3, 2, 4).reshape(NB * 64, 128)
    vmem, hbm = pl.BlockSpec(memory_space=pltpu.VMEM), pl.BlockSpec(memory_space=pl.ANY)
    dma = pltpu.SemaphoreType.DMA
    out = pl.pallas_call(
        kernel,
        out_shape=jax.ShapeDtypeStruct((MEMBERS * 32, 128), F32),
        in_specs=[vmem] * 4 + [hbm] * 3,
        out_specs=hbm,
        scratch_shapes=[
            pltpu.VMEM((MEMBERS * 32, 128), F32),
            pltpu.VMEM((FL, MEMBERS, WIDTH), F32),
            pltpu.VMEM((NB, 128, NOBS), BF16),
            pltpu.VMEM((NB, NOBS, WIDTH), BF16),
            pltpu.VMEM((WIDTH, NB * 128), BF16),
            pltpu.VMEM((PAD, NB * 128), F32),
            pltpu.VMEM((NB, NLEV, 16, PAD), F32),
            pltpu.VMEM((NB, PAD, 8), F32),
            pltpu.VMEM((NB, 16, PAD), F32),
            pltpu.VMEM((NLEV, NB, 16, PAD), F32),
            pltpu.VMEM((NB, 4, 4, PAD), F32),
            pltpu.VMEM((NB, NCOL, 4, PAD), F32),
            pltpu.VMEM((4, 8, 4, PAD), F32),
            pltpu.VMEM((NB - 1, 4, 32, PAD), BF16),
            pltpu.VMEM((NB - 1, NCOL, 32, PAD), BF16),
            pltpu.VMEM((2, 32, NOBS), F32),
            pltpu.VMEM((NB, NOBS, PAD), BF16),
            pltpu.VMEM((NB, NOBS, PAD), BF16),
            pltpu.VMEM((NB, PAD, NOBS), BF16),
            pltpu.VMEM((2, NOBS, NOBS), BF16),
            pltpu.VMEM((2, 128, NOBS), BF16),
            pltpu.VMEM((NOBS, PAD), BF16),
            pltpu.VMEM((NOBS, WIDTH), F32),
            pltpu.VMEM((128, NOBS), BF16),
            pltpu.VMEM((FL, PAD, WIDTH), BF16),
            pltpu.VMEM((FL, NOBS, WIDTH), BF16),
            pltpu.VMEM((NOBS, 8), F32),
            pltpu.VMEM((8, NB * 128), F32),
            pltpu.VMEM((NB, 32, 128), BF16),
            pltpu.VMEM((NB - 1, 256, NOBS), BF16),
            pltpu.VMEM((NB, 32, PAD), F32),
            dma((6,)), dma, dma((2,)), dma((2,)),
            dma((NB,)), dma((NB,)), dma((NB,)), dma((NB,)), dma((NB,)), dma((NB,)),
            dma((NB,)), dma((NB,)), dma((NB,)), dma((NB,)), dma((NB,)), dma((NB,)),
            dma((NB,)), dma((NB,)),
        ],
        compiler_params=pltpu.CompilerParams(
            collective_id=0, has_side_effects=True, vmem_limit_bytes=56 * 1024 * 1024),
        cost_estimate=pl.CostEstimate(flops=8 * 335544320, bytes_accessed=8 * 1024 * 1024, transcendentals=0),
    )(
        jnp.transpose(obs_tile, (0, 2, 1)), obs_offset, obs_value, weights, state, obs_gain, localize,
    )
    return out.reshape(MEMBERS, 4, 4, 2, 128).transpose(0, 1, 3, 2, 4).reshape(ensemble.shape)


def solution(mesh):
    in_specs = (
        P(None, None, "lev", "col"),
        P(None, None, "lev", None),
        P(),
        P(),
        P(),
        P(None, "lev", None),
        P(None, None, "col"),
    )
    out_specs = P(None, None, "lev", "col")
    return jax.shard_map(shards, mesh=mesh, in_specs=in_specs, out_specs=out_specs, check_vma=False)
```

```python
import jax
import jax.numpy as jnp
from jax import lax
from jax.experimental import pallas as pl
from jax.experimental.pallas import tpu as pltpu
from jax.sharding import PartitionSpec as P

F32, BF16, I32 = jnp.float32, jnp.bfloat16, jnp.int32
MESH = pl.DeviceIdType.MESH
MEMBERS = 80
PAD = 128
NB = 4
NOBS = 1024
NCOL, NLEV = 32, 8
FL = 8
WIDTH = 512


def iota(shape, axis):
    return lax.broadcasted_iota(I32, shape, axis)


def dot(a, b):
    return lax.dot_general(a, b, (((1,), (0,)), ((), ())), preferred_element_type=F32)


def dot_nt(a, b):
    return lax.dot_general(a, b, (((1,), (1,)), ((), ())), preferred_element_type=F32)


def parts(x, count):
    out = []
    for _ in range(count):
        piece = x.astype(BF16)
        out.append(piece)
        x = x - piece.astype(F32)
    return out


def wait_bytes(ref, sem):
    pltpu.make_async_copy(ref, ref, sem).wait()


def push(src, dst, s_sem, r_sem, col, lev):
    pltpu.make_async_remote_copy(
        src_ref=src, dst_ref=dst, send_sem=s_sem, recv_sem=r_sem,
        device_id={"col": col, "lev": lev}, device_id_type=MESH).start()


def loop(count, body, unroll=1):
    lax.fori_loop(0, count, lambda k, c: (body(k), c)[1], 0, unroll=unroll)


def kernel(
    tile_ref, off_ref, val_ref, w_ref, ens_hbm, gain_hbm, loc_hbm, out_hbm,
    raw, cur, gain, loc, oh, x, xt, got_t, own, rs, zs, zr, ls, lsend, lrecv, later, inn, an, inc, perm, gainp,
    aj, locs, dt, sa, coef, gcol, wsl, cmat, cbig, ovs,
    in_sem, out_sem, rs_s, rs_r, z_s, z_r, l_s, l_r, wi_s, wi_r, wa_s, wa_r,
    fi_s, fi_r, fa_s, fa_r, ic_s, ic_r, lq_s, lq_r,
):
    col, lev = lax.axis_index("col"), lax.axis_index("lev")
    z, quad = col // 4, col % 4
    x_lo, core = quad // 2, quad % 2
    sibling = col + 1 - 2 * core
    spot = lev * 2 + x_lo
    rho = core * 16 + spot

    loads = [pltpu.make_async_copy(ens_hbm, raw, in_sem.at[0]),
             pltpu.make_async_copy(gain_hbm, gain, in_sem.at[1])]
    loads += [pltpu.make_async_copy(loc_hbm.at[b], loc.at[b], in_sem.at[2 + b]) for b in range(NB)]
    for load in loads:
        load.start()

    px, py = (lev % 2) * 2 + x_lo, lev // 2
    plane = sorted([(dx, dy) for dx in range(4) for dy in range(4)], key=lambda d: -min(d[0], 4 - d[0]) - min(d[1], 4 - d[1]))[:15]

    def moved(dx, dy):
        tx, ty = (px + dx) % 4, (py + dy) % 4
        return z * 4 + (tx % 2) * 2 + core, ty * 2 + tx // 2

    chips = [moved(dx, dy) for dx, dy in plane]
    lev_peers = [moved(dx, dy)[1] for dx, dy in plane if dx % 2 == 0]

    barrier = pltpu.get_barrier_semaphore()

    def greet_col(k):
        pl.semaphore_signal(barrier, inc=1, device_id={"col": lax.rem(col + k + 1, NCOL), "lev": lev}, device_id_type=MESH)

    loop(NCOL - 1, greet_col)
    for c, l in chips:
        pl.semaphore_signal(barrier, inc=1, device_id={"col": c, "lev": l}, device_id_type=MESH)

    tiles = [tile_ref[b] for b in range(NB)]
    member_of = jnp.concatenate(
        [jnp.where(tiles[b] == iota((NCOL, NOBS), 0), 1.0, 0.0) for b in range(NB)], axis=0)
    member_b = member_of.astype(BF16)
    upper = jnp.where(iota((256, 256), 0) < iota((256, 256), 1), 1.0, 0.0).astype(BF16)
    ones = jnp.ones((256, 256), BF16)
    before, total = [], jnp.zeros((128, 256), F32)
    for k in range(4):
        block = member_b[:, 256 * k:256 * (k + 1)]
        before.append(dot(block, upper) + total)
        total = total + dot(block, ones)
    before = jnp.concatenate(before, axis=1)
    row, lane = iota((128, 128), 0), iota((128, 128), 1)
    lower = jnp.where((row // 32 == lane // 32) & (lane < row), 1.0, 0.0).astype(BF16)
    start = dot(lower, total[:, :128].astype(BF16))[:, :1]
    g_rows, code_rows = [], []
    for b in range(NB):
        mine = member_of[32 * b:32 * b + 32]
        begin = start[32 * b:32 * b + 32]
        g = jnp.sum(mine * (before[32 * b:32 * b + 32] + begin), axis=0, keepdims=True)
        g_rows.append(g)
        gi = g.astype(I32)
        first = jnp.sum(mine * begin, axis=0, keepdims=True).astype(I32)
        res = gi & 31
        rank = (gi >> 5) - ((first - res + 31) >> 5)
        slot = 16 * ((res >> 1) & 7) + 8 * (res & 1) + 4 * (res >> 4) + rank
        code_rows.append(jnp.where(tiles[b] == col, slot, -1))

    for b in range(NB):
        pick = jnp.where(code_rows[b] == iota((PAD, NOBS), 0), 1.0, 0.0).astype(BF16)
        off = off_ref[b:b + 1, :]
        head = jnp.concatenate(
            [(off >> 8).astype(F32), (off & 255).astype(F32), jnp.ones((1, NOBS), F32), jnp.zeros((5, NOBS), F32)], axis=0)
        weights = jnp.concatenate(
            [jnp.concatenate([w_ref[pl.ds(64 * b + 2 * c + l, 4, stride=16), :] for l in range(2)], axis=0)
             for c in range(8)], axis=1)
        wp = [p.astype(F32) for p in parts(weights, 3)]
        got = dot_nt(jnp.concatenate([head] + wp, axis=0).astype(BF16), pick)
        column = got[0:1] * 256.0 + got[1:2] + (got[2:3] - 1.0) * 10000.0
        wsl[:, 128 * b:128 * b + 128] = got[8:16] + got[16:24] + got[24:32]
        oh[:, 128 * b:128 * b + 128] = jnp.where(
            iota((WIDTH, PAD), 0) == column.astype(I32), 1.0, 0.0).astype(BF16)
        got_t[b] = jnp.broadcast_to(column, (8, PAD)).T

    x[...] = jnp.zeros_like(x)
    loads[0].wait()

    def rows_of(fl, c):
        return pl.ds((fl % 4) * 8 + fl // 4 + 2 * c, MEMBERS, stride=32)

    def project(fl):
        block = jnp.concatenate([raw[rows_of(fl, c), :] for c in range(4)], axis=1)
        cur[fl] = block
        sa[fl, 0:MEMBERS, :] = (block - jnp.mean(block, axis=0, keepdims=True)).astype(BF16)
        got = dot(jnp.concatenate(parts(block, 3), axis=0), oh[...])
        x[0:MEMBERS, :] += (got[0:80] + got[80:160] + got[160:240]) * wsl[pl.ds(fl, 1), :]

    sa[...] = jnp.zeros_like(sa)
    loop(FL, project, 2)
    for b in range(NB):
        xt[b] = x[:, 128 * b:128 * b + 128].T.reshape(NLEV, 16, PAD)

    pl.semaphore_wait(barrier, NCOL - 1 + 15)

    for to in lev_peers:
        push(xt.at[0, to], rs.at[lev, 0], rs_s.at[0], rs_r.at[0], col, to)
    for to in lev_peers:
        push(xt.at[pl.ds(1, 3), to], rs.at[lev, pl.ds(1, 3)], rs_s.at[1], rs_r.at[1], col, to)

    gcol[...] = jnp.concatenate(g_rows + [jnp.zeros((4, NOBS), F32)], axis=0).T
    inc[...] = jnp.zeros_like(inc)

    def place(b):
        want = ((iota((256, NOBS), 1) & 31) * 32 + (iota((256, NOBS), 1) >> 5)).astype(F32)

        def rows(k):
            at = pl.ds(pl.multiple_of(k * 256, 256), 256)
            perm[b, at, :] = jnp.where(gcol[at, b:b + 1] == want, 1.0, 0.0).astype(BF16)

        loop(4, rows, 2)
        gainp[b] = dot(gain[b], perm[b]).astype(BF16)

    loads[1].wait()
    place(0)

    mine16 = pl.ds(pl.multiple_of(lev * 16, 16), 16)
    here = [jnp.where(got_t[b, mine16, 0:1].astype(I32) == iota((16, WIDTH), 1), 1.0, 0.0) for b in range(1, NB)]
    for b in range(NB - 1):
        loads[2 + b].wait()
        got = dot_nt(jnp.concatenate(here[b:], axis=0).astype(BF16), loc[b])
        if b + 2 < NB:
            later[b, 0:16 * (NB - 2 - b), :] = got[16:]
        for k in range(4):
            for c in range(8):
                ls[k, c] = got[4 * k:4 * k + 4, 128 * c:128 * c + 128]
        lsend[b] = ls[...].reshape(4, 32, PAD).astype(BF16)

    counts = dot_nt(jnp.ones((8, NOBS), BF16), member_b)
    counts = jnp.where(iota((8, 128), 1) // 32 == iota((8, 128), 0), counts, 0.0).astype(BF16)

    def edges(lanes, per_tile):
        at, of = iota((128, lanes), 0) % 32, iota((128, lanes), 1) // per_tile
        low = dot(counts, jnp.where(at < of, 1.0, 0.0).astype(BF16)).astype(I32)
        high = dot(counts, jnp.where(at <= of, 1.0, 0.0).astype(BF16)).astype(I32)
        return low, high

    low, high = edges(128, 4)
    q = iota((32, 128), 0)
    for b in range(NB):
        want = (iota((32, 128), 1) & 3) + ((low[b:b + 1] - rho + 31) >> 5)
        cmat[b] = jnp.where((q == want) & (32 * q + rho < high[b:b + 1]), 1.0, 0.0).astype(BF16)
        is_here = g_rows[b].astype(I32) == 32 * iota((32, NOBS), 0) + rho
        ovs[b] = jnp.broadcast_to(jnp.sum(jnp.where(is_here, val_ref[b:b + 1, :], 0.0), axis=1, keepdims=True), (32, PAD))

    def far_col(k):
        return (col + 16 + ((k + 1) // 2) * (1 - 2 * (k % 2))) % NCOL

    def send_z(b):
        zr[b, col] = zs[b, quad]

        def one(k):
            to = far_col(k)
            push(zs.at[b, to % 4], zr.at[b, col], z_s.at[b], z_r.at[b], to, lev)

        loop(NCOL - 1, one)

    lrecv[:, col] = lsend[:, quad]
    for k in range(1, 4):
        to = (quad + k) % 4
        push(lsend.at[:, to], lrecv.at[:, col], lq_s, lq_r, z * 4 + to, lev)

    def send_l(b):
        piece = lrecv.at[b, pl.ds(z * 4, 4)]
        for k in (4, 3, 5, 2, 6, 1, 7):
            push(piece, piece, l_s.at[b], l_r.at[b], (z + k) % 8 * 4 + quad, lev)

    wait_bytes(rs.at[pl.ds(0, 7), 0], rs_r.at[0])
    rs[lev, 0] = xt[0, lev]
    first = jnp.sum(rs[:, 0], axis=0)
    for k in range(4):
        zs[0, k] = first[4 * k:4 * k + 4]
    send_z(0)
    wait_bytes(rs.at[pl.ds(0, 7), pl.ds(1, 3)], rs_r.at[1])
    for b in range(1, NB):
        rs[lev, b] = xt[b, lev]
        own[b] = jnp.sum(rs[:, b], axis=0)
    for k in range(4):
        zs[1, k] = own[1, 4 * k:4 * k + 4]
    send_z(1)
    wait_bytes(lrecv.at[:, pl.ds(0, 3)], lq_r)
    send_l(0)

    low, high = edges(NOBS, 32)
    row_q, row_c = iota((256, NOBS), 0) % 32, iota((256, NOBS), 0) // 32
    lane_c, lane_r = (iota((256, NOBS), 1) >> 2) & 7, iota((256, NOBS), 1) & 3
    for b in range(1, NB):
        want = lane_r + ((low[b:b + 1] - rho + 31) >> 5)
        hit = (row_q == want) & (row_c == lane_c) & (32 * row_q + rho < high[b:b + 1])
        cbig[b - 1] = jnp.where(hit, 1.0, 0.0).astype(BF16)

    lane_of = iota((32, PAD), 1)
    in_members = lane_of < MEMBERS

    def spread(buf, b, s_sem, r_sem):
        piece = buf.at[b, pl.ds(pl.multiple_of(rho * 32, 32), 32)]
        for c, l in chips:
            push(piece, piece, s_sem.at[b], r_sem.at[b], c, l)

    def forward(buf, b, r_sem, fs_sem, fr_sem):
        wait_bytes(buf.at[b, pl.ds(0, 480)], r_sem.at[b])
        half = buf.at[b, pl.ds(pl.multiple_of(core * 512, 512), 512)]
        push(half, half, fs_sem.at[b], fr_sem.at[b], sibling, lev)

    def anomaly(fl):
        block = cur[fl]
        sa[fl, 0:MEMBERS, :] = (block - jnp.mean(block, axis=0, keepdims=True)).astype(BF16)

    def cov(b, fl):
        for h in range(2):
            at = slice(256 * h, 256 * h + 256)
            got = dot(aj[...], sa[fl, :, at]) * locs[:, at]
            coef[fl, :, at] = got.astype(BF16)

    def change(b, fl):
        cur[fl] += dot(inc[b, 0:MEMBERS, :], coef[fl])

    def gather_z(b):
        wait_bytes(zr.at[b, pl.ds(0, NCOL - 1)], z_r.at[b])
        hi, lo = parts(zr[b].reshape(128, PAD), 2)
        return dot(cmat[b], hi) + dot(cmat[b], lo)

    def centred(v):
        mean = jnp.sum(v, axis=1, keepdims=True) * (1.0 / MEMBERS)
        return jnp.where(iota(v.shape, 1) < MEMBERS, v - mean, 0.0)

    for b in range(1, NB):
        place(b)
    prior = gather_z(0)
    for b in range(NB):
        mine = pl.ds(pl.multiple_of(rho * 32, 32), 32)
        inn[b, mine, :] = jnp.where(in_members, ovs[b] - prior, 0.0).astype(BF16)
        spread(inn, b, wi_s, wi_r)
        anom = centred(prior)
        variance = jnp.sum(anom * anom, axis=1, keepdims=True) / (MEMBERS - 1) + 1e-6
        scale = parts(1.0 / ((MEMBERS - 1) * variance), 3)
        for k in range(3):
            anom = jnp.where(lane_of == MEMBERS + k, scale[k].astype(F32), anom)
        an[b, mine, :] = anom.astype(BF16)
        spread(an, b, wa_s, wa_r)
        if b > 0:
            if b + 1 < NB:
                send_z(b + 1)
            loop(FL, lambda fl: change(b - 1, fl), 4)
            loop(FL, anomaly, 2)
        forward(inn, b, wi_r, fi_s, fi_r)
        near = pl.ds(pl.multiple_of(core * 512, 512), 512)
        away = pl.ds(pl.multiple_of(512 - core * 512, 512), 512)
        rows = dot(gainp[b, :, near], inn[b, near, :])
        wait_bytes(inn.at[b, pl.ds(0, 512)], fi_r.at[b])
        rows = rows + dot(gainp[b, :, away], inn[b, away, :])
        lanes = pl.ds(pl.multiple_of(lev * 128, 128), 128)
        inc[b, 0:MEMBERS, lanes] = rows.T[0:MEMBERS].astype(BF16)
        piece = inc.at[b, pl.ds(0, MEMBERS), lanes]
        for to in lev_peers:
            push(piece, piece, ic_s.at[b], ic_r.at[b], col, to)
        forward(an, b, wa_r, fa_s, fa_r)
        if b + 2 < NB:
            send_l(b + 1)
        wait_bytes(an.at[b, pl.ds(0, 512)], fa_r.at[b])

        def unpack(k):
            at = pl.ds(pl.multiple_of(k * 256, 256), 256)
            got = dot(perm[b, at, :], an[b])
            scale_col = got[:, 80:81] + got[:, 81:82] + got[:, 82:83]
            aj[at, :] = got.astype(BF16)
            locs[at, :] = loc[b, at, :].astype(F32) * scale_col

        if b == NB - 1:
            loads[2 + b].wait()
        loop(4, unpack, 4)
        if b + 1 < NB:
            after = 16 * (NB - 2 - b)
            held = gather_z(b + 1)
            wait_bytes(lrecv.at[b, pl.ds(0, 28)], l_r.at[b])
            sel = dot(cbig[b], lrecv[b].reshape(NOBS, PAD))
            sel = jnp.concatenate([sel[32 * c:32 * c + 32] for c in range(8)], axis=1)
            if after:
                slots = own[b + 2:NB].reshape(after, PAD)
                held = jnp.concatenate([held, slots], axis=0)
                sel = jnp.concatenate([sel, later[b, 0:after, :]], axis=0)
            xh, xl = parts(centred(held), 2)
            pull = jnp.where((iota((16, PAD), 1) >= MEMBERS) & (iota((16, PAD), 1) < MEMBERS + 3), 1.0, 0.0).astype(BF16)
            count = 32 + after
            got = dot_nt(jnp.concatenate([xh, xl, pull], axis=0), aj[...])
            d = (got[0:count] + got[count:2 * count]) * got[2 * count:2 * count + 1] * sel
            dh, dl = parts(d, 2)
            dt[0:count, :] = dh
            dt[count:2 * count, :] = dl
        loop(FL, lambda fl: cov(b, fl), 4)
        wait_bytes(inc.at[b, pl.ds(0, MEMBERS), pl.ds(0, 896)], ic_r.at[b])
        if b + 1 < NB:
            got = dot_nt(dt[0:2 * count, :], inc[b])
            held = held + got[0:count] + got[count:2 * count]
            prior = held[0:32]
            if after:
                own[b + 2:NB] = held[32:].reshape(NB - 2 - b, 16, PAD)
                for k in range(4):
                    zs[b + 2, k] = held[32 + 4 * k:36 + 4 * k]

    def finish(fl):
        block = cur[fl] + dot(inc[NB - 1, 0:MEMBERS, :], coef[fl])
        for c in range(4):
            raw[rows_of(fl, c), :] = block[:, 128 * c:128 * c + 128]

    loop(FL, finish, 4)
    done = pltpu.make_async_copy(raw, out_hbm, out_sem)
    done.start()
    wait_bytes(rs.at[pl.ds(0, 7), 0], rs_s.at[0])
    wait_bytes(rs.at[pl.ds(0, 7), pl.ds(1, 3)], rs_s.at[1])
    wait_bytes(lrecv.at[:, pl.ds(0, 3)], lq_s)
    for b in range(NB):
        wait_bytes(zr.at[b, pl.ds(0, NCOL - 1)], z_s.at[b])
        if b + 1 < NB:
            wait_bytes(lrecv.at[b, pl.ds(0, 28)], l_s.at[b])
        wait_bytes(inn.at[b, pl.ds(0, 480)], wi_s.at[b])
        wait_bytes(an.at[b, pl.ds(0, 480)], wa_s.at[b])
        wait_bytes(inn.at[b, pl.ds(0, 512)], fi_s.at[b])
        wait_bytes(an.at[b, pl.ds(0, 512)], fa_s.at[b])
        wait_bytes(inc.at[b, pl.ds(0, MEMBERS), pl.ds(0, 896)], ic_s.at[b])
    done.wait()


def shards(ensemble, obs_weight, obs_value, obs_tile, obs_offset, obs_gain, localize):
    state = ensemble.reshape(MEMBERS, 4, 2, 4, 128).transpose(0, 1, 3, 2, 4).reshape(MEMBERS * 32, 128)
    weights = obs_weight.reshape(NB, 4, 2, 8, 128).transpose(0, 1, 3, 2, 4).reshape(NB * 64, 128)
    vmem, hbm = pl.BlockSpec(memory_space=pltpu.VMEM), pl.BlockSpec(memory_space=pl.ANY)
    dma = pltpu.SemaphoreType.DMA
    out = pl.pallas_call(
        kernel,
        out_shape=jax.ShapeDtypeStruct((MEMBERS * 32, 128), F32),
        in_specs=[vmem] * 4 + [hbm] * 3,
        out_specs=hbm,
        scratch_shapes=[
            pltpu.VMEM((MEMBERS * 32, 128), F32),
            pltpu.VMEM((FL, MEMBERS, WIDTH), F32),
            pltpu.VMEM((NB, 128, NOBS), BF16),
            pltpu.VMEM((NB, NOBS, WIDTH), BF16),
            pltpu.VMEM((WIDTH, NB * 128), BF16),
            pltpu.VMEM((PAD, NB * 128), F32),
            pltpu.VMEM((NB, NLEV, 16, PAD), F32),
            pltpu.VMEM((NB, PAD, 8), F32),
            pltpu.VMEM((NB, 16, PAD), F32),
            pltpu.VMEM((NLEV, NB, 16, PAD), F32),
            pltpu.VMEM((NB, 4, 4, PAD), F32),
            pltpu.VMEM((NB, NCOL, 4, PAD), F32),
            pltpu.VMEM((4, 8, 4, PAD), F32),
            pltpu.VMEM((NB - 1, 4, 32, PAD), BF16),
            pltpu.VMEM((NB - 1, NCOL, 32, PAD), BF16),
            pltpu.VMEM((2, 32, NOBS), F32),
            pltpu.VMEM((NB, NOBS, PAD), BF16),
            pltpu.VMEM((NB, NOBS, PAD), BF16),
            pltpu.VMEM((NB, PAD, NOBS), BF16),
            pltpu.VMEM((NB, NOBS, NOBS), BF16),
            pltpu.VMEM((NB, 128, NOBS), BF16),
            pltpu.VMEM((NOBS, PAD), BF16),
            pltpu.VMEM((NOBS, WIDTH), F32),
            pltpu.VMEM((128, NOBS), BF16),
            pltpu.VMEM((FL, PAD, WIDTH), BF16),
            pltpu.VMEM((FL, NOBS, WIDTH), BF16),
            pltpu.VMEM((NOBS, 8), F32),
            pltpu.VMEM((8, NB * 128), F32),
            pltpu.VMEM((NB, 32, 128), BF16),
            pltpu.VMEM((NB - 1, 256, NOBS), BF16),
            pltpu.VMEM((NB, 32, PAD), F32),
            dma((6,)), dma, dma((2,)), dma((2,)),
            dma((NB,)), dma((NB,)), dma((NB,)), dma((NB,)), dma((NB,)), dma((NB,)),
            dma((NB,)), dma((NB,)), dma((NB,)), dma((NB,)), dma((NB,)), dma((NB,)),
            dma((NB,)), dma((NB,)), dma, dma,
        ],
        compiler_params=pltpu.CompilerParams(
            collective_id=0, has_side_effects=True, vmem_limit_bytes=56 * 1024 * 1024),
        cost_estimate=pl.CostEstimate(flops=8 * 335544320, bytes_accessed=8 * 1024 * 1024, transcendentals=0),
    )(
        jnp.transpose(obs_tile, (0, 2, 1)), obs_offset, obs_value, weights, state, obs_gain, localize,
    )
    return out.reshape(MEMBERS, 4, 4, 2, 128).transpose(0, 1, 3, 2, 4).reshape(ensemble.shape)


def solution(mesh):
    in_specs = (
        P(None, None, "lev", "col"),
        P(None, None, "lev", None),
        P(),
        P(),
        P(),
        P(None, "lev", None),
        P(None, None, "col"),
    )
    out_specs = P(None, None, "lev", "col")
    return jax.shard_map(shards, mesh=mesh, in_specs=in_specs, out_specs=out_specs, check_vma=False)
```
